32 devices in a mesh: ref: 2 (over y), dat: 16 (over z, x, core).
Axes of the slice: x: 2, y: 2, z: 4, core: 2. Of those that a mesh axis runs over, the one named last changes fastest.
Arguments:
- particles: bfloat16 [1024, 16384], P('dat'), may hold values from -64 to 64
- references: bfloat16 [2, 72, 16384], P(None, 'ref'), may hold values from -0.046875 to 0.046875
- normalizers: float32 [2, 72], P(None, 'ref'), may hold values from 0 to 3
- class_order: int32 [2], replicated, may hold values from 0 to 1, each once
- shift_offsets: int32 [9, 2], replicated, may hold values from -4 to 4, as said below
Outputs:
- class_sums: float32 [2, 72, 16384], P(None, 'ref', 'dat')
- evidence: float32 [2, 1024], P(None, 'dat')
The draws below stay inside these ranges and needn't reach their ends.
Inputs may be any that keep to these rules, and one draw needn't show every extreme that they name: `shift_offsets`: the nine offset pairs are the grid the finite set (-4, 0, 4) x the finite set (-s, 0, s) for some s of 1 to 4, row offset first; all pairs differ.
All inputs are finite; a program needn't handle non-finite values.
Results may differ from the reference program's by a relative error of at most 0.0027.
Values sent between devices are 32-bit elements; how exact they have to be, the bound alone decides.
A program may use at most 128 MiB of HBM per device.

```python
import math
import jax
import jax.numpy as jnp
from jax import lax

SIDE = 128
ROT = 72
SHIFTS = 9
CLASSES = 2
PARTICLES = 1024


def shared_references(key):
    values = jax.random.truncated_normal(key, -6.0, 6.0, (CLASSES, ROT, SIDE * SIDE), jnp.float32)
    return values / SIDE


def draw_references(key, part):
    return shared_references(key).astype(jnp.bfloat16)


def draw_particles(key, part):
    key = jax.random.fold_in(key, 7)
    noise_key, scale_key = jax.random.split(key, 2)
    row_scales = jnp.exp(jax.random.uniform(scale_key, (PARTICLES, 1), jnp.float32, math.log(0.3), math.log(3.0)))
    noise = jax.random.truncated_normal(noise_key, -6.0, 6.0, (PARTICLES, SIDE * SIDE), jnp.float32)
    values = noise * row_scales
    return values.astype(jnp.bfloat16)


def draw_shift_offsets(key, part):
    key = jax.random.fold_in(key, 5)
    column_step = jax.random.randint(key, (), 1, 5).astype(jnp.int32)
    steps_base = jnp.array([-1, 0, 1], jnp.int32)
    row_part = jnp.repeat(steps_base * 4, 3)
    column_part = jnp.tile(steps_base, 3) * column_step
    return jnp.stack([row_part, column_part], axis=1).astype(jnp.int32)


def level_of(stream_key, extent, pieces, least, top_value):
    level, own = 1.0, jax.random.fold_in(stream_key, 6)
    for dim, parts in pieces:
        draws = jnp.exp(jax.random.uniform(jax.random.fold_in(own, dim), (parts,), jnp.float32, least / len(pieces), top_value / len(pieces)))
        level = level * jnp.repeat(draws, extent[dim] // parts).reshape([-1 if axis == dim else 1 for axis in range(len(extent))])
    return level


def setup_inputs(seed: int = 0) -> dict:
    streams_of = jax.random.split(jax.random.key(seed), 6)
    particles = draw_particles(jax.random.fold_in(streams_of[5], 71), 0)
    references = draw_references(jax.random.fold_in(streams_of[5], 71), 0)
    normalizers = jnp.clip(3.0 * jax.random.uniform(streams_of[2], (CLASSES, ROT), jnp.float32) ** level_of(streams_of[2], (CLASSES, ROT), ((1, 2),), -0.2, 0.2), 0.0, 3.0)
    class_order = jax.random.permutation(streams_of[3], CLASSES).astype(jnp.int32)
    shift_offsets = draw_shift_offsets(jax.random.fold_in(streams_of[5], 71), 0)
    return {"particles": particles, "references": references, "normalizers": normalizers, "class_order": class_order, "shift_offsets": shift_offsets}


def shifted_table(class_refs, shift_offsets):
    images = class_refs.reshape(ROT, SIDE, SIDE)
    moved_refs = [jnp.roll(images, (shift_offsets[shift_index, 0], shift_offsets[shift_index, 1]), axis=(1, 2)) for shift_index in range(SHIFTS)]
    return jnp.stack(moved_refs, axis=1).reshape(ROT * SHIFTS, SIDE * SIDE)

def align_back(weighted, shift_offsets):
    weighted_grids = weighted.reshape(ROT, SHIFTS, SIDE, SIDE)
    result = jnp.zeros((ROT, SIDE, SIDE), jnp.float32)
    for shift_index in range(SHIFTS):
        result = result + jnp.roll(weighted_grids[:, shift_index], (-shift_offsets[shift_index, 0], -shift_offsets[shift_index, 1]), axis=(1, 2))
    return result.reshape(ROT, SIDE * SIDE)

def reference(particles, references, normalizers, class_order, shift_offsets):
    norm_scale = float(ROT) / math.sqrt(PARTICLES)
    class_sums = []
    evidence = []
    for step_index in range(CLASSES):
        chosen = class_order[step_index]
        class_refs = references[chosen]
        shift_table = shifted_table(class_refs, shift_offsets)
        scores = lax.dot_general(particles, shift_table, (((1,), (1,)), ((), ())), preferred_element_type=jnp.float32)
        scores = scores.reshape(PARTICLES, ROT, SHIFTS) - normalizers[chosen][None, :, None]
        highest = lax.optimization_barrier(jnp.max(scores, axis=(1, 2)))
        shifted_exp = jnp.exp(scores - highest[:, None, None])
        partition = lax.optimization_barrier(jnp.sum(shifted_exp, axis=(1, 2)))
        weights = (shifted_exp / partition[:, None, None]).astype(jnp.bfloat16).reshape(PARTICLES, ROT * SHIFTS)
        weighted = lax.dot_general(weights, particles, (((0,), (0,)), ((), ())), preferred_element_type=jnp.float32)
        class_sums.append(align_back(weighted, shift_offsets) * norm_scale)
        evidence.append(highest + jnp.log(partition))
    return (jnp.stack(class_sums), jnp.stack(evidence))
```

```python
import functools
import math

import jax
import jax.numpy as jnp
from jax import lax
from jax.experimental import pallas as pl
from jax.experimental.pallas import tpu as pltpu
from jax.sharding import PartitionSpec as P

SIDE = 128
PIXELS = SIDE * SIDE
CLASSES = 2
ROW_STEP = 4
EDGE = ROW_STEP * SIDE
MESH = pl.DeviceIdType.MESH
FAR = 1e30


def stage_of(slot):
    return (slot & -slot).bit_length() - 1


def kernel(
    n_ref, n_dat, norm_scale,
    order_ref, shift_ref, norm_ref, part_ref, refs_ref,
    sums_ref, evid_ref,
    moved, table, scores, weights, acc, inbox, stats_out, stats_in,
    send_sem, recv_sem, stat_send, stat_recv,
):
    count = part_ref.shape[0]
    rots = refs_ref.shape[1]
    pad = table.shape[0] // CLASSES
    block = acc.shape[2]
    my_ref = lax.axis_index("ref")
    me = lax.axis_index("dat")
    stages = n_dat.bit_length() - 1
    bits = [lax.rem(me // (1 << s), 2) for s in range(stages)]

    def partner(s):
        return me + (1 << s) * (1 - 2 * bits[s])

    barrier = pltpu.get_barrier_semaphore()
    for s in range(stages):
        pl.semaphore_signal(barrier, inc=1, device_id=(my_ref, partner(s)), device_id_type=MESH)
    for o in range(1, n_ref):
        pl.semaphore_signal(
            barrier, inc=1, device_id=(lax.rem(my_ref + o, n_ref), me), device_id_type=MESH
        )

    step = shift_ref[0, 1]
    for k in range(1, shift_ref.shape[0]):
        step = jnp.maximum(step, shift_ref[k, 1])
    source = lax.broadcasted_iota(jnp.int32, (SIDE, SIDE), 0)
    target = lax.broadcasted_iota(jnp.int32, (SIDE, SIDE), 1)
    distance = source - target
    up = jnp.where((distance == step) | (distance == step - SIDE), 1.0, 0.0)
    down = jnp.where((distance == -step) | (distance == SIDE - step), 1.0, 0.0)
    permute = jnp.concatenate([up, down], axis=1).astype(jnp.bfloat16)
    tile_group = 8

    def move(g, carry):
        for j in range(tile_group):
            at = pl.multiple_of((g * tile_group + j) * SIDE, SIDE)
            piece = part_ref[:, pl.ds(at, SIDE)]
            both = jnp.dot(piece, permute, preferred_element_type=jnp.float32).astype(jnp.bfloat16)
            moved[0:count, pl.ds(EDGE + at, SIDE)] = piece
            moved[count : 2 * count, pl.ds(EDGE + at, SIDE)] = both[:, :SIDE]
            moved[2 * count : 3 * count, pl.ds(EDGE + at, SIDE)] = both[:, SIDE:]
        return carry

    lax.fori_loop(0, SIDE // tile_group, move, 0)
    moved[:, 0:EDGE] = moved[:, PIXELS : PIXELS + EDGE]
    moved[:, EDGE + PIXELS : 2 * EDGE + PIXELS] = moved[:, EDGE : 2 * EDGE]

    low = (rots // 16) * 16
    for c in range(CLASSES):
        if low < pad:
            table[c * pad + low : (c + 1) * pad, :] = jnp.zeros(
                (pad - low, table.shape[1]), jnp.bfloat16
            )
        table[c * pad : c * pad + rots, EDGE : EDGE + PIXELS] = refs_ref[c]
    table[:, 0:EDGE] = table[:, PIXELS : PIXELS + EDGE]
    table[:, EDGE + PIXELS : 2 * EDGE + PIXELS] = table[:, EDGE : 2 * EDGE]

    scores[...] = jnp.zeros_like(scores)
    depth = 2048

    def score(g, carry):
        at = pl.multiple_of(g * depth, depth)
        left = jnp.concatenate([table[:, pl.ds(at + a * EDGE, depth)] for a in range(3)], axis=0)
        right = moved[:, pl.ds(EDGE + at, depth)]
        scores[...] += lax.dot_general(
            left, right, (((1,), (1,)), ((), ())), preferred_element_type=jnp.float32
        )
        return carry

    lax.fori_loop(0, PIXELS // depth, score, 0)

    eye = lax.broadcasted_iota(jnp.int32, (rots, rots), 0) == lax.broadcasted_iota(
        jnp.int32, (rots, rots), 1
    )

    def fold(row, op):
        return op(op(row[:, 0:count], row[:, count : 2 * count]), row[:, 2 * count : 3 * count])

    def spread(row):
        return jnp.concatenate([row, row, row], axis=1)

    stats_out[...] = jnp.zeros_like(stats_out)
    exps = []
    highs = []
    totals = []
    for c in range(CLASSES):
        norm_column = jnp.sum(
            jnp.where(eye, norm_ref[c : c + 1, :], 0.0), axis=1, keepdims=True
        )
        parts = [
            scores[(a * CLASSES + c) * pad : (a * CLASSES + c) * pad + rots, :] - norm_column
            for a in range(3)
        ]
        best = jnp.maximum(jnp.maximum(parts[0], parts[1]), parts[2])
        high = fold(jnp.max(best, axis=0, keepdims=True), jnp.maximum)
        wide = spread(high)
        grown = [jnp.exp(p - wide) for p in parts]
        total = fold(jnp.sum(grown[0] + grown[1] + grown[2], axis=0, keepdims=True), jnp.add)
        exps.append(grown)
        highs.append(high)
        totals.append(total)
        stats_out[c : c + 1, 0:count] = high
        stats_out[CLASSES + c : CLASSES + c + 1, 0:count] = total

    pl.semaphore_wait(barrier, stages + n_ref - 1)
    notes = []
    for o in range(1, n_ref):
        note = pltpu.make_async_remote_copy(
            src_ref=stats_out,
            dst_ref=stats_in.at[o - 1],
            send_sem=stat_send.at[o - 1],
            recv_sem=stat_recv.at[o - 1],
            device_id=(lax.rem(my_ref + o, n_ref), me),
            device_id_type=MESH,
        )
        note.start()
        notes.append(note)
    for note in notes:
        note.wait()

    first = order_ref[0] == 0
    finals = []
    evidence = []
    for c in range(CLASSES):
        high = highs[c]
        for o in range(1, n_ref):
            high = jnp.maximum(high, stats_in[o - 1, c : c + 1, 0:count])
        mine = jnp.exp(highs[c] - high)
        total = totals[c] * mine
        for o in range(1, n_ref):
            total = total + stats_in[o - 1, CLASSES + c : CLASSES + c + 1, 0:count] * jnp.exp(
                stats_in[o - 1, c : c + 1, 0:count] - high
            )
        factor = spread(mine / total)
        finals.append([e * factor for e in exps[c]])
        evidence.append(high + jnp.log(total))
    evid_ref[0:1, :] = jnp.where(first, evidence[0], evidence[1])
    evid_ref[1:2, :] = jnp.where(first, evidence[1], evidence[0])
    width = 3 * count
    for a in range(3):
        one, two = finals[0][a], finals[1][a]
        ordered = jnp.concatenate(
            [jnp.where(first, one, two), jnp.where(first, two, one)], axis=0
        )
        weights[a] = ordered.astype(jnp.bfloat16)

    def compute(slot):
        owner = me
        for s in range(stages):
            if (slot >> s) & 1:
                owner = owner + (1 << s) * (1 - 2 * bits[s])
        at = pl.multiple_of(owner * block, block)
        total = jnp.dot(
            weights[0], moved[:, pl.ds(at + 2 * EDGE, block)], preferred_element_type=jnp.float32
        )
        total = total + jnp.dot(
            weights[1], moved[:, pl.ds(at + EDGE, block)], preferred_element_type=jnp.float32
        )
        acc[slot] = total + jnp.dot(
            weights[2], moved[:, pl.ds(at, block)], preferred_element_type=jnp.float32
        )

    copies = {}
    missing = {slot: stage_of(slot) if slot else stages for slot in range(n_dat)}

    def send(slot):
        s = stage_of(slot)
        copies[slot] = pltpu.make_async_remote_copy(
            src_ref=acc.at[slot],
            dst_ref=inbox.at[slot],
            send_sem=send_sem.at[slot],
            recv_sem=recv_sem.at[slot],
            device_id=(my_ref, partner(s)),
            device_id_type=MESH,
        )
        copies[slot].start()

    def finish(slot):
        into = slot & (slot - 1)
        copies[slot].wait_recv()
        acc[into] = acc[into] + inbox[slot]
        missing[into] -= 1
        if into and missing[into] == 0:
            send(into)

    odd = sorted(range(1, n_dat, 2), key=lambda slot: (-(slot & 2), -slot))
    for place, slot in enumerate(odd):
        compute(slot)
        send(slot)
        compute(slot - 1)
        if place:
            finish(odd[place - 1])
    finish(odd[-1])
    rest = sorted(
        range(2, n_dat, 2), key=lambda slot: (slot <= n_dat // 2, stage_of(slot), -slot)
    )
    for slot in rest:
        finish(slot)
    for slot in range(1, n_dat):
        copies[slot].wait_send()
    for c in range(CLASSES):
        sums_ref[c] = acc[0, c * rots : (c + 1) * rots, :] * norm_scale


def per_device(n_ref, n_dat, particles, references, normalizers, class_order, shift_offsets):
    count = particles.shape[0]
    rots = references.shape[1]
    block = PIXELS // n_dat
    pad = -(-rots // 16) * 16
    rows = CLASSES * rots
    norm_scale = float(rots * n_ref) / math.sqrt(count * n_dat)
    smem = pl.BlockSpec(memory_space=pltpu.SMEM)
    vmem = pl.BlockSpec(memory_space=pltpu.VMEM)
    return pl.pallas_call(
        functools.partial(kernel, n_ref, n_dat, norm_scale),
        out_shape=(
            jax.ShapeDtypeStruct((CLASSES, rots, block), jnp.float32),
            jax.ShapeDtypeStruct((CLASSES, count), jnp.float32),
        ),
        in_specs=[smem, smem, vmem, vmem, vmem],
        out_specs=(vmem, vmem),
        scratch_shapes=[
            pltpu.VMEM((3 * count, PIXELS + 2 * EDGE), jnp.bfloat16),
            pltpu.VMEM((CLASSES * pad, PIXELS + 2 * EDGE), jnp.bfloat16),
            pltpu.VMEM((3 * CLASSES * pad, 3 * count), jnp.float32),
            pltpu.VMEM((3, rows, 3 * count), jnp.bfloat16),
            pltpu.VMEM((n_dat, rows, block), jnp.float32),
            pltpu.VMEM((n_dat, rows, block), jnp.float32),
            pltpu.VMEM((8, 128), jnp.float32),
            pltpu.VMEM((max(n_ref - 1, 1), 8, 128), jnp.float32),
            pltpu.SemaphoreType.DMA((n_dat,)),
            pltpu.SemaphoreType.DMA((n_dat,)),
            pltpu.SemaphoreType.DMA((max(n_ref - 1, 1),)),
            pltpu.SemaphoreType.DMA((max(n_ref - 1, 1),)),
        ],
        compiler_params=pltpu.CompilerParams(
            collective_id=0, has_side_effects=True, vmem_limit_bytes=48 * 1024 * 1024
        ),
    )(class_order, shift_offsets, normalizers, particles, references)


def solution(mesh):
    return jax.shard_map(
        functools.partial(per_device, mesh.shape["ref"], mesh.shape["dat"]),
        mesh=mesh,
        in_specs=(P("dat", None), P(None, "ref", None), P(None, "ref"), P(), P()),
        out_specs=(P(None, "ref", "dat"), P(None, "dat")),
        check_vma=False,
    )
```

```python
import functools
import math

import jax
import jax.numpy as jnp
from jax import lax
from jax.experimental import pallas as pl
from jax.experimental.pallas import tpu as pltpu
from jax.sharding import PartitionSpec as P

SIDE = 128
PIXELS = SIDE * SIDE
CLASSES = 2
ROW_STEP = 4
EDGE = ROW_STEP * SIDE
MESH = pl.DeviceIdType.MESH


def stage_of(slot):
    return (slot & -slot).bit_length() - 1


def whole_plan(n):
    plan = []
    for t in range(CLASSES):
        if t:
            plan += [("score", t, 0), ("weigh", t, 0)]
        odd = range(n - 1, 0, -2)
        for slot in odd:
            plan += [("calc", t, slot), ("calc", t, slot - 1)]
        plan += [("take", t, slot) for slot in odd]
    rest = sorted(range(2, n, 2), key=lambda slot: (stage_of(slot), -slot))
    return plan + [("take", t, slot) for slot in rest for t in range(CLASSES)]


PLAN16 = (
    ("c", 0, 15), ("c", 0, 14), ("c", 0, 11), ("t", 0, 15), ("c", 0, 10), ("c", 0, 7),
    ("t", 0, 11), ("c", 0, 6), ("c", 0, 13), ("t", 0, 7), ("c", 0, 12), ("c", 0, 9),
    ("c", 0, 8), ("c", 0, 5), ("c", 0, 4), ("t", 0, 13), ("t", 0, 9), ("t", 0, 5),
    ("s", 1, 0), ("t", 0, 14), ("c", 0, 3), ("c", 0, 2), ("c", 0, 1), ("c", 0, 0),
    ("t", 0, 1), ("w", 1, 0),
    ("c", 1, 15), ("c", 1, 14), ("c", 1, 11), ("t", 1, 15), ("c", 1, 10), ("c", 1, 7),
    ("t", 1, 11), ("c", 1, 6), ("c", 1, 3), ("t", 1, 7), ("t", 0, 3), ("t", 0, 10),
    ("t", 0, 12),
    ("c", 1, 2), ("c", 1, 13), ("c", 1, 12), ("t", 1, 3), ("c", 1, 9), ("c", 1, 8),
    ("t", 1, 13), ("t", 0, 6), ("c", 1, 5), ("c", 1, 4), ("t", 1, 9), ("c", 1, 1),
    ("c", 1, 0), ("t", 1, 1),
    ("t", 1, 6), ("t", 1, 14), ("t", 1, 5), ("t", 1, 10), ("t", 1, 12), ("t", 0, 2),
    ("t", 0, 4), ("t", 0, 8), ("t", 1, 4), ("t", 1, 2), ("t", 1, 8),
)


def plan_of(n):
    if n != 16:
        return whole_plan(n), {}
    names = {"c": "calc", "t": "take", "s": "score", "w": "weigh"}
    steps = [(names[kind], t, slot) for kind, t, slot in PLAN16]
    return steps, {(1, 6): (2, 2)}


def kernel(
    n_ref, n_dat, norm_scale,
    order_ref, shift_ref, norm_ref, part_ref, refs_ref,
    sums_ref, evid_ref,
    moved, table, scores, grown, weights, acc, inbox, stats_out, stats_in,
    send_sem, recv_sem, stat_send, stat_recv,
):
    count = part_ref.shape[0]
    rots = refs_ref.shape[1]
    pad = table.shape[0]
    block = acc.shape[3]
    my_ref = lax.axis_index("ref")
    me = lax.axis_index("dat")
    stages = n_dat.bit_length() - 1
    bits = [lax.rem(me // (1 << s), 2) for s in range(stages)]

    def partner(s):
        return me + (1 << s) * (1 - 2 * bits[s])

    barrier = pltpu.get_barrier_semaphore()
    for s in range(stages):
        pl.semaphore_signal(barrier, inc=1, device_id=(my_ref, partner(s)), device_id_type=MESH)
    for o in range(1, n_ref):
        pl.semaphore_signal(
            barrier, inc=1, device_id=(lax.rem(my_ref + o, n_ref), me), device_id_type=MESH
        )

    step = shift_ref[1, 0]
    for k in range(1, shift_ref.shape[1]):
        step = jnp.maximum(step, shift_ref[1, k])
    source = lax.broadcasted_iota(jnp.int32, (SIDE, SIDE), 0)
    target = lax.broadcasted_iota(jnp.int32, (SIDE, SIDE), 1)
    distance = source - target
    up = jnp.where((distance == step) | (distance == step - SIDE), 1.0, 0.0)
    down = jnp.where((distance == -step) | (distance == SIDE - step), 1.0, 0.0)
    permute = jnp.concatenate([up, down], axis=1).astype(jnp.bfloat16)
    tile_group = 8

    def move(g, carry):
        for j in range(tile_group):
            at = pl.multiple_of((g * tile_group + j) * SIDE, SIDE)
            piece = part_ref[:, pl.ds(at, SIDE)]
            both = jnp.dot(piece, permute, preferred_element_type=jnp.float32).astype(jnp.bfloat16)
            moved[0:count, pl.ds(EDGE + at, SIDE)] = piece
            moved[count : 2 * count, pl.ds(EDGE + at, SIDE)] = both[:, :SIDE]
            moved[2 * count : 3 * count, pl.ds(EDGE + at, SIDE)] = both[:, SIDE:]
        return carry

    lax.fori_loop(0, SIDE // tile_group, move, 0)
    moved[:, 0:EDGE] = moved[:, PIXELS : PIXELS + EDGE]
    moved[:, EDGE + PIXELS : 2 * EDGE + PIXELS] = moved[:, EDGE : 2 * EDGE]

    low = (rots // 16) * 16
    depth = 2048
    eye = lax.broadcasted_iota(jnp.int32, (rots, rots), 0) == lax.broadcasted_iota(
        jnp.int32, (rots, rots), 1
    )

    def fold(row, op):
        return op(op(row[:, 0:count], row[:, count : 2 * count]), row[:, 2 * count : 3 * count])

    def spread(row):
        return jnp.concatenate([row, row, row], axis=1)

    def score_step(t):
        chosen = order_ref[t]
        if low < pad:
            table[low:pad, :] = jnp.zeros((pad - low, table.shape[1]), jnp.bfloat16)
        table[0:rots, EDGE : EDGE + PIXELS] = refs_ref[chosen]
        table[:, 0:EDGE] = table[:, PIXELS : PIXELS + EDGE]
        table[:, EDGE + PIXELS : 2 * EDGE + PIXELS] = table[:, EDGE : 2 * EDGE]

        scores[...] = jnp.zeros_like(scores)

        def score(g, carry):
            at = pl.multiple_of(g * depth, depth)
            left = jnp.concatenate(
                [table[:, pl.ds(at + a * EDGE, depth)] for a in range(3)], axis=0
            )
            right = moved[:, pl.ds(EDGE + at, depth)]
            scores[...] += lax.dot_general(
                left, right, (((1,), (1,)), ((), ())), preferred_element_type=jnp.float32
            )
            return carry

        lax.fori_loop(0, PIXELS // depth, score, 0)
        columns = [
            jnp.sum(jnp.where(eye, norm_ref[c : c + 1, :], 0.0), axis=1, keepdims=True)
            for c in range(CLASSES)
        ]
        norm_column = jnp.where(chosen == 0, columns[0], columns[1])
        parts = [scores[a * pad : a * pad + rots, :] - norm_column for a in range(3)]
        best = jnp.maximum(jnp.maximum(parts[0], parts[1]), parts[2])
        high = fold(jnp.max(best, axis=0, keepdims=True), jnp.maximum)
        wide = spread(high)
        raised = [jnp.exp(p - wide) for p in parts]
        total = fold(jnp.sum(raised[0] + raised[1] + raised[2], axis=0, keepdims=True), jnp.add)
        for a in range(3):
            grown[a] = raised[a]
        stats_out[t] = jnp.zeros((8, 128), jnp.float32)
        stats_out[t, 0:1, 0:count] = high
        stats_out[t, 1:2, 0:count] = total
        if t == 0:
            pl.semaphore_wait(barrier, stages + n_ref - 1)
        notes = []
        for o in range(1, n_ref):
            note = pltpu.make_async_remote_copy(
                src_ref=stats_out.at[t],
                dst_ref=stats_in.at[t, o - 1],
                send_sem=stat_send.at[t, o - 1],
                recv_sem=stat_recv.at[t, o - 1],
                device_id=(lax.rem(my_ref + o, n_ref), me),
                device_id_type=MESH,
            )
            note.start()
            notes.append(note)
        return notes

    def weigh_step(t, notes):
        for note in notes:
            note.wait()
        own = stats_out[t, 0:1, 0:count]
        high = own
        for o in range(1, n_ref):
            high = jnp.maximum(high, stats_in[t, o - 1, 0:1, 0:count])
        mine = jnp.exp(own - high)
        total = stats_out[t, 1:2, 0:count] * mine
        for o in range(1, n_ref):
            total = total + stats_in[t, o - 1, 1:2, 0:count] * jnp.exp(
                stats_in[t, o - 1, 0:1, 0:count] - high
            )
        factor = spread(mine / total)
        for a in range(3):
            weights[t, a] = (grown[a] * factor).astype(jnp.bfloat16)
        evid_ref[t : t + 1, :] = high + jnp.log(total)

    def compute(t, slot):
        owner = me
        for s in range(stages):
            if (slot >> s) & 1:
                owner = owner + (1 << s) * (1 - 2 * bits[s])
        at = pl.multiple_of(owner * block, block)
        total = jnp.dot(
            weights[t, 0], moved[:, pl.ds(at + 2 * EDGE, block)],
            preferred_element_type=jnp.float32,
        )
        total = total + jnp.dot(
            weights[t, 1], moved[:, pl.ds(at + EDGE, block)], preferred_element_type=jnp.float32
        )
        acc[t, slot] = total + jnp.dot(
            weights[t, 2], moved[:, pl.ds(at, block)], preferred_element_type=jnp.float32
        )

    plan, routes = plan_of(n_dat)
    pairs = [(t, slot) for t in range(CLASSES) for slot in range(n_dat)]
    route = {
        (t, slot): routes.get((t, slot), (stage_of(slot), slot & (slot - 1)))
        for t, slot in pairs
        if slot
    }
    missing = {pair: 1 for pair in pairs}
    for (t, slot), (stage, into) in route.items():
        missing[t, into] += 1
    copies = {}

    def ready(t, slot):
        missing[t, slot] -= 1
        if slot == 0 or missing[t, slot]:
            return
        copies[t, slot] = pltpu.make_async_remote_copy(
            src_ref=acc.at[t, slot],
            dst_ref=inbox.at[t, slot],
            send_sem=send_sem.at[t, slot],
            recv_sem=recv_sem.at[t, slot],
            device_id=(my_ref, partner(route[t, slot][0])),
            device_id_type=MESH,
        )
        copies[t, slot].start()

    weigh_step(0, score_step(0))
    notes = None
    for kind, t, slot in plan:
        if kind == "score":
            notes = score_step(t)
        elif kind == "weigh":
            weigh_step(t, notes)
        elif kind == "calc":
            compute(t, slot)
            ready(t, slot)
        else:
            into = route[t, slot][1]
            copies[t, slot].wait_recv()
            acc[t, into] = acc[t, into] + inbox[t, slot]
            ready(t, into)
    for pair in route:
        copies[pair].wait_send()
    for t in range(CLASSES):
        sums_ref[t] = acc[t, 0] * norm_scale


def per_device(n_ref, n_dat, particles, references, normalizers, class_order, shift_offsets):
    count = particles.shape[0]
    rots = references.shape[1]
    block = PIXELS // n_dat
    pad = -(-rots // 16) * 16
    norm_scale = float(rots * n_ref) / math.sqrt(count * n_dat)
    smem = pl.BlockSpec(memory_space=pltpu.SMEM)
    vmem = pl.BlockSpec(memory_space=pltpu.VMEM)
    return pl.pallas_call(
        functools.partial(kernel, n_ref, n_dat, norm_scale),
        out_shape=(
            jax.ShapeDtypeStruct((CLASSES, rots, block), jnp.float32),
            jax.ShapeDtypeStruct((CLASSES, count), jnp.float32),
        ),
        in_specs=[smem, smem, vmem, vmem, vmem],
        out_specs=(vmem, vmem),
        scratch_shapes=[
            pltpu.VMEM((3 * count, PIXELS + 2 * EDGE), jnp.bfloat16),
            pltpu.VMEM((pad, PIXELS + 2 * EDGE), jnp.bfloat16),
            pltpu.VMEM((3 * pad, 3 * count), jnp.float32),
            pltpu.VMEM((3, rots, 3 * count), jnp.float32),
            pltpu.VMEM((CLASSES, 3, rots, 3 * count), jnp.bfloat16),
            pltpu.VMEM((CLASSES, n_dat, rots, block), jnp.float32),
            pltpu.VMEM((CLASSES, n_dat, rots, block), jnp.float32),
            pltpu.VMEM((CLASSES, 8, 128), jnp.float32),
            pltpu.VMEM((CLASSES, max(n_ref - 1, 1), 8, 128), jnp.float32),
            pltpu.SemaphoreType.DMA((CLASSES, n_dat)),
            pltpu.SemaphoreType.DMA((CLASSES, n_dat)),
            pltpu.SemaphoreType.DMA((CLASSES, max(n_ref - 1, 1))),
            pltpu.SemaphoreType.DMA((CLASSES, max(n_ref - 1, 1))),
        ],
        compiler_params=pltpu.CompilerParams(
            collective_id=0, has_side_effects=True, vmem_limit_bytes=48 * 1024 * 1024
        ),
    )(class_order, shift_offsets.T, normalizers, particles, references)


def solution(mesh):
    return jax.shard_map(
        functools.partial(per_device, mesh.shape["ref"], mesh.shape["dat"]),
        mesh=mesh,
        in_specs=(P("dat", None), P(None, "ref", None), P(None, "ref"), P(), P()),
        out_specs=(P(None, "ref", "dat"), P(None, "dat")),
        check_vma=False,
    )
```

```python
import functools
import math

import jax
import jax.numpy as jnp
from jax import lax
from jax.experimental import pallas as pl
from jax.experimental.pallas import tpu as pltpu
from jax.sharding import PartitionSpec as P

SIDE = 128
PIXELS = SIDE * SIDE
CLASSES = 2
ROW_STEP = 4
EDGE = ROW_STEP * SIDE
MESH = pl.DeviceIdType.MESH


def stage_of(slot):
    return (slot & -slot).bit_length() - 1


def kernel(
    n_ref, n_dat, norm_scale,
    order_ref, shift_ref, norm_ref, part_ref, refs_ref,
    sums_ref, evid_ref,
    moved, table, scores, weights, acc, inbox, stats_out, stats_in,
    send_sem, recv_sem, stat_send, stat_recv,
):
    count = part_ref.shape[0]
    rots = refs_ref.shape[1]
    pad = table.shape[0] // CLASSES
    block = acc.shape[2]
    my_ref = lax.axis_index("ref")
    me = lax.axis_index("dat")
    stages = n_dat.bit_length() - 1
    bits = [lax.rem(me // (1 << s), 2) for s in range(stages)]

    def partner(s):
        return me + (1 << s) * (1 - 2 * bits[s])

    barrier = pltpu.get_barrier_semaphore()
    for s in range(stages):
        pl.semaphore_signal(barrier, inc=1, device_id=(my_ref, partner(s)), device_id_type=MESH)
    for o in range(1, n_ref):
        pl.semaphore_signal(
            barrier, inc=1, device_id=(lax.rem(my_ref + o, n_ref), me), device_id_type=MESH
        )

    step = shift_ref[1, 0]
    for k in range(1, shift_ref.shape[1]):
        step = jnp.maximum(step, shift_ref[1, k])
    source = lax.broadcasted_iota(jnp.int32, (SIDE, SIDE), 0)
    target = lax.broadcasted_iota(jnp.int32, (SIDE, SIDE), 1)
    distance = source - target
    up = jnp.where((distance == step) | (distance == step - SIDE), 1.0, 0.0)
    down = jnp.where((distance == -step) | (distance == SIDE - step), 1.0, 0.0)
    permute = jnp.concatenate([up, down], axis=1).astype(jnp.bfloat16)
    tile_group = 8

    def move(g, carry):
        for j in range(tile_group):
            at = pl.multiple_of((g * tile_group + j) * SIDE, SIDE)
            piece = part_ref[:, pl.ds(at, SIDE)]
            both = jnp.dot(piece, permute, preferred_element_type=jnp.float32).astype(jnp.bfloat16)
            moved[0:count, pl.ds(EDGE + at, SIDE)] = piece
            moved[count : 2 * count, pl.ds(EDGE + at, SIDE)] = both[:, :SIDE]
            moved[2 * count : 3 * count, pl.ds(EDGE + at, SIDE)] = both[:, SIDE:]
        return carry

    lax.fori_loop(0, SIDE // tile_group, move, 0)
    moved[:, 0:EDGE] = moved[:, PIXELS : PIXELS + EDGE]
    moved[:, EDGE + PIXELS : 2 * EDGE + PIXELS] = moved[:, EDGE : 2 * EDGE]

    low = (rots // 16) * 16
    for c in range(CLASSES):
        if low < pad:
            table[c * pad + low : (c + 1) * pad, :] = jnp.zeros(
                (pad - low, table.shape[1]), jnp.bfloat16
            )
        table[c * pad : c * pad + rots, EDGE : EDGE + PIXELS] = refs_ref[c]
    table[:, 0:EDGE] = table[:, PIXELS : PIXELS + EDGE]
    table[:, EDGE + PIXELS : 2 * EDGE + PIXELS] = table[:, EDGE : 2 * EDGE]

    scores[...] = jnp.zeros_like(scores)
    depth = 2048

    def score(g, carry):
        at = pl.multiple_of(g * depth, depth)
        left = jnp.concatenate([table[:, pl.ds(at + a * EDGE, depth)] for a in range(3)], axis=0)
        right = moved[:, pl.ds(EDGE + at, depth)]
        scores[...] += lax.dot_general(
            left, right, (((1,), (1,)), ((), ())), preferred_element_type=jnp.float32
        )
        return carry

    lax.fori_loop(0, PIXELS // depth, score, 0)

    eye = lax.broadcasted_iota(jnp.int32, (rots, rots), 0) == lax.broadcasted_iota(
        jnp.int32, (rots, rots), 1
    )

    def fold(row, op):
        return op(op(row[:, 0:count], row[:, count : 2 * count]), row[:, 2 * count : 3 * count])

    def spread(row):
        return jnp.concatenate([row, row, row], axis=1)

    stats_out[...] = jnp.zeros_like(stats_out)
    exps = []
    highs = []
    totals = []
    for c in range(CLASSES):
        norm_column = jnp.sum(
            jnp.where(eye, norm_ref[c : c + 1, :], 0.0), axis=1, keepdims=True
        )
        parts = [
            scores[(a * CLASSES + c) * pad : (a * CLASSES + c) * pad + rots, :] - norm_column
            for a in range(3)
        ]
        best = jnp.maximum(jnp.maximum(parts[0], parts[1]), parts[2])
        high = fold(jnp.max(best, axis=0, keepdims=True), jnp.maximum)
        wide = spread(high)
        grown = [jnp.exp(p - wide) for p in parts]
        total = fold(jnp.sum(grown[0] + grown[1] + grown[2], axis=0, keepdims=True), jnp.add)
        exps.append(grown)
        highs.append(high)
        totals.append(total)
        stats_out[c : c + 1, 0:count] = high
        stats_out[CLASSES + c : CLASSES + c + 1, 0:count] = total

    pl.semaphore_wait(barrier, stages + n_ref - 1)
    notes = []
    for o in range(1, n_ref):
        note = pltpu.make_async_remote_copy(
            src_ref=stats_out,
            dst_ref=stats_in.at[o - 1],
            send_sem=stat_send.at[o - 1],
            recv_sem=stat_recv.at[o - 1],
            device_id=(lax.rem(my_ref + o, n_ref), me),
            device_id_type=MESH,
        )
        note.start()
        notes.append(note)
    for note in notes:
        note.wait()

    first = order_ref[0] == 0
    finals = []
    evidence = []
    for c in range(CLASSES):
        high = highs[c]
        for o in range(1, n_ref):
            high = jnp.maximum(high, stats_in[o - 1, c : c + 1, 0:count])
        mine = jnp.exp(highs[c] - high)
        total = totals[c] * mine
        for o in range(1, n_ref):
            total = total + stats_in[o - 1, CLASSES + c : CLASSES + c + 1, 0:count] * jnp.exp(
                stats_in[o - 1, c : c + 1, 0:count] - high
            )
        factor = spread(mine / total)
        finals.append([e * factor for e in exps[c]])
        evidence.append(high + jnp.log(total))
    evid_ref[0:1, :] = jnp.where(first, evidence[0], evidence[1])
    evid_ref[1:2, :] = jnp.where(first, evidence[1], evidence[0])
    width = 3 * count
    for a in range(3):
        one, two = finals[0][a], finals[1][a]
        ordered = jnp.concatenate(
            [jnp.where(first, one, two), jnp.where(first, two, one)], axis=0
        )
        weights[a] = ordered.astype(jnp.bfloat16)

    def compute(slot):
        owner = me
        for s in range(stages):
            if (slot >> s) & 1:
                owner = owner + (1 << s) * (1 - 2 * bits[s])
        at = pl.multiple_of(owner * block, block)
        total = jnp.dot(
            weights[0], moved[:, pl.ds(at + 2 * EDGE, block)], preferred_element_type=jnp.float32
        )
        total = total + jnp.dot(
            weights[1], moved[:, pl.ds(at + EDGE, block)], preferred_element_type=jnp.float32
        )
        acc[slot] = total + jnp.dot(
            weights[2], moved[:, pl.ds(at, block)], preferred_element_type=jnp.float32
        )

    copies = {}
    missing = {slot: stage_of(slot) if slot else stages for slot in range(n_dat)}

    def send(slot):
        s = stage_of(slot)
        copies[slot] = pltpu.make_async_remote_copy(
            src_ref=acc.at[slot],
            dst_ref=inbox.at[slot],
            send_sem=send_sem.at[slot],
            recv_sem=recv_sem.at[slot],
            device_id=(my_ref, partner(s)),
            device_id_type=MESH,
        )
        copies[slot].start()

    def finish(slot):
        into = slot & (slot - 1)
        copies[slot].wait_recv()
        acc[into] = acc[into] + inbox[slot]
        missing[into] -= 1
        if into and missing[into] == 0:
            send(into)

    odd = sorted(range(1, n_dat, 2), key=lambda slot: (-(slot & 2), -slot))
    for place, slot in enumerate(odd):
        compute(slot)
        send(slot)
        compute(slot - 1)
        if place:
            finish(odd[place - 1])
    finish(odd[-1])
    rest = sorted(
        range(2, n_dat, 2), key=lambda slot: (slot <= n_dat // 2, stage_of(slot), -slot)
    )
    for slot in rest:
        finish(slot)
    for slot in range(1, n_dat):
        copies[slot].wait_send()
    for c in range(CLASSES):
        sums_ref[c] = acc[0, c * rots : (c + 1) * rots, :] * norm_scale


def per_device(n_ref, n_dat, particles, references, normalizers, class_order, shift_offsets):
    count = particles.shape[0]
    rots = references.shape[1]
    block = PIXELS // n_dat
    pad = -(-rots // 16) * 16
    rows = CLASSES * rots
    norm_scale = float(rots * n_ref) / math.sqrt(count * n_dat)
    smem = pl.BlockSpec(memory_space=pltpu.SMEM)
    vmem = pl.BlockSpec(memory_space=pltpu.VMEM)
    return pl.pallas_call(
        functools.partial(kernel, n_ref, n_dat, norm_scale),
        out_shape=(
            jax.ShapeDtypeStruct((CLASSES, rots, block), jnp.float32),
            jax.ShapeDtypeStruct((CLASSES, count), jnp.float32),
        ),
        in_specs=[smem, smem, vmem, vmem, vmem],
        out_specs=(vmem, vmem),
        scratch_shapes=[
            pltpu.VMEM((3 * count, PIXELS + 2 * EDGE), jnp.bfloat16),
            pltpu.VMEM((CLASSES * pad, PIXELS + 2 * EDGE), jnp.bfloat16),
            pltpu.VMEM((3 * CLASSES * pad, 3 * count), jnp.float32),
            pltpu.VMEM((3, rows, 3 * count), jnp.bfloat16),
            pltpu.VMEM((n_dat, rows, block), jnp.float32),
            pltpu.VMEM((n_dat, rows, block), jnp.float32),
            pltpu.VMEM((8, 128), jnp.float32),
            pltpu.VMEM((max(n_ref - 1, 1), 8, 128), jnp.float32),
            pltpu.SemaphoreType.DMA((n_dat,)),
            pltpu.SemaphoreType.DMA((n_dat,)),
            pltpu.SemaphoreType.DMA((max(n_ref - 1, 1),)),
            pltpu.SemaphoreType.DMA((max(n_ref - 1, 1),)),
        ],
        compiler_params=pltpu.CompilerParams(
            collective_id=0, has_side_effects=True, vmem_limit_bytes=48 * 1024 * 1024
        ),
    )(class_order, shift_offsets.T, normalizers, particles, references)


def solution(mesh):
    return jax.shard_map(
        functools.partial(per_device, mesh.shape["ref"], mesh.shape["dat"]),
        mesh=mesh,
        in_specs=(P("dat", None), P(None, "ref", None), P(None, "ref"), P(), P()),
        out_specs=(P(None, "ref", "dat"), P(None, "dat")),
        check_vma=False,
    )
```
